32 devices in a mesh: grp: 2 (over y), seq: 4 (over z), tp: 2 (over x), sub: 2 (over core).
Axes of the slice: x: 2, y: 2, z: 4, core: 2. Of those that a mesh axis runs over, the one named last changes fastest.
Arguments:
- acts: bfloat16 [16384, 4096], P(('grp', 'seq', 'sub'), 'tp'), parts along dimension 0, may hold values from -6 to 6
- out_grads: bfloat16 [16384, 14336], P(('grp', 'seq', 'sub'), 'tp'), parts along dimension 0, may hold values from -6 to 6
- proj_in: bfloat16 [4096, 64], P('tp'), may hold values from -0.09375 to 0.09375
- proj_out: bfloat16 [14336, 64], P('tp'), may hold values from -0.046875 to 0.046875
- seq_lengths: int32 [16, 16], P(('grp', 'seq', 'sub')), parts along dimension 0, may hold values from 1 to 256, 1024 in all within a row
- hard_ids: int32 [16, 8], P(('grp', 'seq', 'sub')), parts along dimension 0, may hold values from 0 to 15
- slots: int32 [128], P(('grp', 'seq', 'sub')), parts along dimension 0, may hold values from 0 to 63, each once
Outputs:
- features: float32 [128, 4096], P(('grp', 'seq', 'sub'), 'tp'), parts along dimension 0
The draws below stay inside these ranges and needn't reach their ends.
There are 2 independent parts, one for each index of `grp`. The reference program is written for one: setup_inputs(seed, part) draws one part's arguments, and reference() takes and returns one part's arrays. A program takes and returns all parts, laid end to end along the dimension named above; an argument that names none is the same for every part. Nothing has to cross between parts.
Inputs may be any that keep to these rules, and one draw needn't show every extreme that they name: `slots`: each example's row, every row once. `hard_ids`: repeats allowed.
All inputs are finite; a program needn't handle non-finite values.
Results may differ from the reference program's by a relative error of at most 0.0003.
Values sent between devices are 32-bit elements; how exact they have to be, the bound alone decides.
A program may use at most 64 MiB of HBM per device.

```python
import math
import jax
import jax.numpy as jnp
import numpy as np
from jax import lax

D = 4096
FF = 14336
RANK = 64
TOK_DEV = 1024
SEQ_DEV = 16
HARD_DEV = 8
MOST = 256
DEVS = 8
TOKENS = 8192
EXAMPLES = 64


def place_ends(values, own_key, least, largest):
    extent = values.shape
    spot = [jax.random.randint(jax.random.fold_in(own_key, axis), (), 0, extent[axis]) for axis in range(len(extent))]
    values = values.at[tuple(spot)].set(least)
    longest = extent.index(max(extent))
    spot[longest] = (spot[longest] + 1) % extent[longest]
    return values.at[tuple(spot)].set(largest)


def steps_of(stream_key, dims, split, smallest, high):
    level = 1.0
    for axis_at, blocks in split:
        heights = jax.random.uniform(jax.random.fold_in(jax.random.fold_in(stream_key, 6), axis_at), (blocks,), jnp.float32, smallest / len(split), high / len(split))
        level = level * jnp.repeat(jnp.exp(heights), dims[axis_at] // blocks).reshape((-1,) + (1,) * (len(dims) - 1 - axis_at))
    return level


def length_profile(count, total, most, skew):
    weights = [(1 << 20) // math.isqrt(standing ** skew) + 1 for standing in range(2, count + 1)]
    rest, given = total - most - (count - 1), [1] * (count - 1)
    while rest > 0:
        free = [i for i in range(count - 1) if given[i] < most]
        mass, left = sum([weights[i] for i in free]), rest
        for i in free:
            addition = min(most - given[i], max(1, left * weights[i] // mass), rest)
            given[i] = given[i] + addition
            rest = rest - addition
    return np.array([most] + given)


def uneven_parts(key, number_of, total, most, slope):
    if number_of == 2:
        one = jax.random.randint(key, (), max(1, total - most), min(most, total - 1) + 1)
        return jnp.stack([one, total - one])
    tallies = jnp.asarray(length_profile(number_of, total, most, slope), jnp.int32)
    twos = (number_of - 1) // 2
    source_of, taker = tallies[1:1 + 2 * twos:2], tallies[2:2 + 2 * twos:2]
    room = jnp.minimum(source_of - 1, most - taker)
    shifted = jax.random.randint(jax.random.fold_in(key, 1), (twos,), 0, 1 << 20) % (room + 1)
    tallies = tallies.at[1:1 + 2 * twos:2].set(source_of - shifted).at[2:2 + 2 * twos:2].set(taker + shifted)
    return tallies[jax.random.permutation(jax.random.fold_in(key, 2), number_of)]


def noise(own_key, shape, deviation, limit, pieces=(), kind=jnp.bfloat16):
    result = deviation * jax.random.normal(own_key, shape, jnp.float32)
    if pieces:
        result = result * steps_of(own_key, shape, pieces, -0.22, 0.18)
    return jnp.clip(result, -limit, limit).astype(kind)


def setup_inputs(seed: int = 0, part: int = 0) -> dict:
    seeds = jax.random.split(jax.random.key(seed), 8)
    part_keys = jax.random.split(jax.random.fold_in(seeds[7], part), 8)
    acts = noise(part_keys[0], (TOKENS, D), 1.0, 6.0, ((0, 8), (1, 2)))
    out_grads = noise(part_keys[1], (TOKENS, FF), 1.0, 6.0, ((0, 8), (1, 2)))
    proj_in = noise(seeds[2], (D, RANK), D ** -0.5, 0.09375, ((0, 2),))
    proj_out = noise(seeds[3], (FF, RANK), FF ** -0.5, 0.046875, ((0, 2),))
    seq_lengths = jax.vmap(lambda own: uneven_parts(own, SEQ_DEV, TOK_DEV, MOST, 1))(jax.random.split(part_keys[4], DEVS)).reshape((DEVS, SEQ_DEV)).astype(jnp.int32)
    hard_ids = place_ends(jax.random.randint(part_keys[5], (DEVS, HARD_DEV), 0, SEQ_DEV), jax.random.fold_in(part_keys[5], 1), 0, SEQ_DEV - 1).astype(jnp.int32)
    slots = jax.random.permutation(part_keys[6], EXAMPLES).astype(jnp.int32)
    return dict(acts=acts, out_grads=out_grads, proj_in=proj_in, proj_out=proj_out, seq_lengths=seq_lengths, hard_ids=hard_ids, slots=slots)


def reference(acts, out_grads, proj_in, proj_out, seq_lengths, hard_ids, slots):
    proj_acts = jnp.dot(acts, proj_in, preferred_element_type=jnp.float32)
    proj_grads = jnp.dot(out_grads, proj_out, preferred_element_type=jnp.float32)
    acts_blocks = proj_acts.reshape(DEVS, TOK_DEV, RANK)
    grad_blocks = proj_grads.reshape(DEVS, TOK_DEV, RANK)
    ends = jnp.cumsum(seq_lengths, axis=1)
    starts = ends - seq_lengths
    first = jnp.take_along_axis(starts, hard_ids, axis=1)
    after = jnp.take_along_axis(ends, hard_ids, axis=1)
    position = jnp.arange(TOK_DEV, dtype=jnp.int32)
    masks = ((position[None, None, :] >= first[:, :, None]) & (position[None, None, :] < after[:, :, None])).astype(jnp.float32)

    def one_block(items):
        mask, left, right = items
        return jnp.einsum("kt,ti,tj->kij", mask, left, right, precision=lax.Precision.HIGHEST)

    gradient = lax.map(one_block, (masks, acts_blocks, grad_blocks))
    flat = gradient.reshape(EXAMPLES, RANK * RANK)
    return jnp.zeros((EXAMPLES, RANK * RANK), jnp.float32).at[slots].set(flat)
```

```python
import jax
import jax.numpy as jnp
from jax import lax
from jax.experimental import pallas as pl
from jax.experimental.pallas import tpu as pltpu
from jax.sharding import PartitionSpec as P

MESH = pl.DeviceIdType.MESH
CHUNK = 256


def project(rows, turned):
    return lax.dot_general(
        rows, turned, (((1,), (1,)), ((), ())), preferred_element_type=jnp.float32
    )


def kernel(
    n_seq, n_sub, n_tp,
    acts, grads, w_in, w_out, lengths, ids, slots,
    out,
    acts_v, grads_v, w_in_v, w_out_v,
    a_own, a_got, g_own, g_got, acc, gath, slot_all,
    load_sem, a_send, a_recv, g_send, g_recv, s_send, s_recv, f_send, f_recv, h_send,
):
    seq, sub, tp = lax.axis_index("seq"), lax.axis_index("sub"), lax.axis_index("tp")
    ranks = n_seq * n_sub
    rank = seq * n_sub + sub
    chunks = acts.shape[0] // CHUNK
    share = a_own.shape[2]
    hard = ids.shape[1]
    count = lengths.shape[1]
    half = CHUNK // 2
    rank_full = w_in.shape[0]

    load_w_in = pltpu.make_async_copy(w_in, w_in_v, load_sem.at[0])
    load_w_out = pltpu.make_async_copy(w_out, w_out_v, load_sem.at[1])
    load_acts, load_grads = [], []
    for c in range(chunks):
        rows = pl.ds(c * CHUNK, CHUNK)
        load_acts.append(pltpu.make_async_copy(acts.at[rows], acts_v.at[rows], load_sem.at[2 + c]))
        load_grads.append(
            pltpu.make_async_copy(grads.at[rows], grads_v.at[rows], load_sem.at[2 + chunks + c])
        )
    load_w_in.start()
    for copy in load_acts:
        copy.start()
    load_w_out.start()
    for copy in load_grads:
        copy.start()

    barrier = pltpu.get_barrier_semaphore()
    for d in range(1, n_tp):
        pl.semaphore_signal(
            barrier, inc=1, device_id={"tp": lax.rem(tp + d, n_tp)}, device_id_type=MESH
        )
    for d in range(1, ranks):
        peer = lax.rem(rank + d, ranks)
        pl.semaphore_signal(
            barrier,
            inc=1,
            device_id={"seq": peer // n_sub, "sub": lax.rem(peer, n_sub)},
            device_id_type=MESH,
        )
    firsts = [jnp.int32(0)] * hard
    afters = [jnp.int32(0)] * hard
    chosen = [ids[0, k] for k in range(hard)]
    start = jnp.int32(0)
    for s in range(count):
        end = start + lengths[0, s]
        for k in range(hard):
            firsts[k] = jnp.where(chosen[k] == s, start, firsts[k])
            afters[k] = jnp.where(chosen[k] == s, end, afters[k])
        start = end
    tile_lane = lax.broadcasted_iota(jnp.int32, slot_all.shape[1:], 1)
    tile = jnp.full(slot_all.shape[1:], -1, jnp.int32)
    for k in range(hard):
        tile = jnp.where(tile_lane == rank * hard + k, slots[k], tile)
    slot_all[rank] = tile
    pl.semaphore_wait(barrier, n_tp - 1 + ranks - 1)

    slot_copies = []
    for d in range(1, ranks):
        peer = lax.rem(rank + d, ranks)
        copy = pltpu.make_async_remote_copy(
            src_ref=slot_all.at[rank],
            dst_ref=slot_all.at[rank],
            send_sem=s_send.at[d - 1],
            recv_sem=s_recv.at[d - 1],
            device_id={"seq": peer // n_sub, "sub": lax.rem(peer, n_sub)},
            device_id_type=MESH,
        )
        copy.start()
        slot_copies.append(copy)

    a_copies, g_copies = [], []
    load_w_in.wait()
    for c in range(chunks):
        load_acts[c].wait()
        part = project(acts_v[c * CHUNK:(c + 1) * CHUNK, :], w_in_v[...])
        turned = part.T
        for q in range(n_tp):
            a_own[c, q] = turned[q * share:(q + 1) * share, :]
        for d in range(1, n_tp):
            to = lax.rem(tp + d, n_tp)
            copy = pltpu.make_async_remote_copy(
                src_ref=a_own.at[c, to],
                dst_ref=a_got.at[d - 1, c],
                send_sem=a_send.at[d - 1, c],
                recv_sem=a_recv.at[d - 1, c],
                device_id={"tp": to},
                device_id_type=MESH,
            )
            copy.start()
            a_copies.append(copy)
    load_w_out.wait()
    for c in range(chunks):
        load_grads[c].wait()
        part = project(grads_v[c * CHUNK:(c + 1) * CHUNK, :], w_out_v[...])
        g_own[c] = jnp.concatenate([part[:half], part[half:]], axis=1)
        for d in range(1, n_tp):
            copy = pltpu.make_async_remote_copy(
                src_ref=g_own.at[c],
                dst_ref=g_got.at[d - 1, c],
                send_sem=g_send.at[d - 1, c],
                recv_sem=g_recv.at[d - 1, c],
                device_id={"tp": lax.rem(tp + d, n_tp)},
                device_id_type=MESH,
            )
            copy.start()
            g_copies.append(copy)

    for copy in slot_copies:
        copy.wait()
    every = slot_all[0]
    for other in range(1, ranks):
        every = jnp.maximum(every, slot_all[other])
    wanted = rank * hard + lax.broadcasted_iota(jnp.int32, every.shape, 0)
    picker = jnp.where(every == wanted, 1.0, 0.0)[:, :ranks * hard].astype(jnp.bfloat16)

    position = lax.broadcasted_iota(jnp.int32, (share, CHUNK), 1)
    lane = lax.broadcasted_iota(jnp.int32, (half, 2 * rank_full), 1)
    for c in range(chunks):
        for d in range(n_tp - 1):
            a_copies[c * (n_tp - 1) + d].wait()
        left = a_own[c, tp]
        for d in range(n_tp - 1):
            left = left + a_got[d, c]
        pieces = []
        for k in range(hard):
            inside = (position >= firsts[k] - c * CHUNK) & (position < afters[k] - c * CHUNK)
            pieces.append(jnp.where(inside, left, 0.0))
        left = jnp.concatenate(pieces, axis=0)
        left_hi = left.astype(jnp.bfloat16)
        left_lo = (left - left_hi.astype(jnp.float32)).astype(jnp.bfloat16)
        for d in range(n_tp - 1):
            g_copies[c * (n_tp - 1) + d].wait()
        pair = g_own[c]
        for d in range(n_tp - 1):
            pair = pair + g_got[d, c]
        swapped = pltpu.roll(pair, rank_full, 1)
        right = jnp.concatenate(
            [jnp.where(lane < rank_full, pair, swapped), jnp.where(lane < rank_full, swapped, pair)],
            axis=0,
        )
        right_hi = right.astype(jnp.bfloat16)
        right_lo = (right - right_hi.astype(jnp.float32)).astype(jnp.bfloat16)
        both = jnp.dot(
            left_hi,
            jnp.concatenate([right_hi, right_lo], axis=1),
            preferred_element_type=jnp.float32,
        )
        total = (
            both[:, :2 * rank_full]
            + both[:, 2 * rank_full:]
            + jnp.dot(left_lo, right_hi, preferred_element_type=jnp.float32)
        )
        if c == 0:
            acc[...] = total
        else:
            acc[...] += total
    out_lane = lax.broadcasted_iota(jnp.int32, (hard, 2 * rank_full), 1)
    mine = pl.ds(pl.multiple_of(rank * hard, hard), hard)
    for j in range(share // 2):
        even = acc[pl.ds(2 * j, hard, stride=share), :]
        odd = acc[pl.ds(2 * j + 1, hard, stride=share), :]
        gath[mine, j * 128:(j + 1) * 128] = jnp.where(out_lane < rank_full, even, odd)

    to_chips, to_cores = [], []
    for d in range(1, n_seq):
        copy = pltpu.make_async_remote_copy(
            src_ref=gath.at[mine],
            dst_ref=gath.at[mine],
            send_sem=f_send.at[d - 1],
            recv_sem=f_recv.at[d - 1],
            device_id={"seq": lax.rem(seq + d, n_seq)},
            device_id_type=MESH,
        )
        copy.start()
        to_chips.append(copy)
    for d in range(n_seq):
        if d:
            to_chips[d - 1].wait_recv()
        owner = lax.rem(seq + n_seq - d, n_seq) * n_sub + sub
        block = pl.ds(pl.multiple_of(owner * hard, hard), hard)
        for b in range(1, n_sub):
            copy = pltpu.make_async_remote_copy(
                src_ref=gath.at[block],
                dst_ref=gath.at[block],
                send_sem=h_send.at[b - 1, 0, d],
                recv_sem=h_send.at[b - 1, 1, d],
                device_id={"sub": lax.rem(sub + b, n_sub)},
                device_id_type=MESH,
            )
            copy.start()
            to_cores.append(copy)
    for copy in to_chips:
        copy.wait_send()
    for copy in to_cores:
        copy.wait()
    every = gath[...]
    high = every.astype(jnp.bfloat16)
    low = (every - high.astype(jnp.float32)).astype(jnp.bfloat16)
    out[...] = jnp.dot(picker, high, preferred_element_type=jnp.float32) + jnp.dot(
        picker, low, preferred_element_type=jnp.float32
    )


def body(acts, grads, w_in, w_out, lengths, ids, slots):
    n_seq, n_sub, n_tp = (lax.axis_size(name) for name in ("seq", "sub", "tp"))
    tokens, features = acts.shape
    hidden = grads.shape[1]
    rank_full = w_in.shape[1]
    w_in, w_out = w_in.T, w_out.T
    share = rank_full // n_tp
    hard = ids.shape[1]
    chunks = tokens // CHUNK
    ranks = n_seq * n_sub
    f32 = jnp.float32
    dma = pltpu.SemaphoreType.DMA
    hbm = pl.BlockSpec(memory_space=pl.ANY)
    smem = pl.BlockSpec(memory_space=pltpu.SMEM)

    def run(*refs):
        kernel(n_seq, n_sub, n_tp, *refs)

    return pl.pallas_call(
        run,
        out_shape=jax.ShapeDtypeStruct((hard, share * rank_full), f32),
        in_specs=[hbm] * 4 + [smem] * 3,
        out_specs=pl.BlockSpec(memory_space=pltpu.VMEM),
        scratch_shapes=[
            pltpu.VMEM((tokens, features), acts.dtype),
            pltpu.VMEM((tokens, hidden), grads.dtype),
            pltpu.VMEM(w_in.shape, w_in.dtype),
            pltpu.VMEM(w_out.shape, w_out.dtype),
            pltpu.VMEM((chunks, n_tp, share, CHUNK), f32),
            pltpu.VMEM((n_tp - 1, chunks, share, CHUNK), f32),
            pltpu.VMEM((chunks, CHUNK // 2, 2 * rank_full), f32),
            pltpu.VMEM((n_tp - 1, chunks, CHUNK // 2, 2 * rank_full), f32),
            pltpu.VMEM((hard * share, 2 * rank_full), f32),
            pltpu.VMEM((ranks * hard, share * rank_full), f32),
            pltpu.VMEM((ranks, hard, -(-ranks * hard // 128) * 128), jnp.int32),
            dma((2 + 2 * chunks,)),
            dma((n_tp - 1, chunks)),
            dma((n_tp - 1, chunks)),
            dma((n_tp - 1, chunks)),
            dma((n_tp - 1, chunks)),
            dma((ranks - 1,)),
            dma((ranks - 1,)),
            dma((n_seq - 1,)),
            dma((n_seq - 1,)),
            dma((n_sub - 1, 2, n_seq)),
        ],
        compiler_params=pltpu.CompilerParams(
            collective_id=0, has_side_effects=True, vmem_limit_bytes=48 * 2**20
        ),
        cost_estimate=pl.CostEstimate(
            flops=2 * tokens * (features + hidden) * rank_full,
            bytes_accessed=2 * tokens * (features + hidden),
            transcendentals=0,
        ),
    )(acts, grads, w_in, w_out, lengths, ids, slots)


def solution(mesh):
    placed = (
        P(("grp", "seq", "sub"), "tp"),
        P(("grp", "seq", "sub"), "tp"),
        P("tp", None),
        P("tp", None),
        P(("grp", "seq", "sub"), None),
        P(("grp", "seq", "sub"), None),
        P(("grp", "seq", "sub")),
    )
    return jax.shard_map(
        body, mesh=mesh, in_specs=placed, out_specs=P(("grp", "seq", "sub"), "tp"), check_vma=False
    )
```

```python
import jax
import jax.numpy as jnp
from jax import lax
from jax.experimental import pallas as pl
from jax.experimental.pallas import tpu as pltpu
from jax.sharding import PartitionSpec as P

MESH = pl.DeviceIdType.MESH
CHUNK = 256


def project(rows, turned):
    return lax.dot_general(
        rows, turned, (((1,), (1,)), ((), ())), preferred_element_type=jnp.float32
    )


def kernel(
    n_seq, n_sub, n_tp,
    acts, grads, w_in, w_out, lengths_in, ids_in, slots_in,
    out,
    acts_v, grads_v, w_in_v, w_out_v, lengths, ids, slots,
    a_own, a_got, g_own, g_got, acc, gath, slot_all,
    load_sem, small_sem, a_send, a_recv, g_send, g_recv, s_send, s_recv, f_send, f_recv, h_send,
):
    seq, sub, tp = lax.axis_index("seq"), lax.axis_index("sub"), lax.axis_index("tp")
    ranks = n_seq * n_sub
    rank = seq * n_sub + sub
    chunks = acts.shape[0] // CHUNK
    share = a_own.shape[2]
    hard = ids.shape[1]
    count = lengths.shape[1]
    half = CHUNK // 2
    rank_full = w_in.shape[0]

    load_w_in = pltpu.make_async_copy(w_in, w_in_v, load_sem.at[0])
    load_w_out = pltpu.make_async_copy(w_out, w_out_v, load_sem.at[1])
    load_acts, load_grads = [], []
    for c in range(chunks):
        rows = pl.ds(c * CHUNK, CHUNK)
        load_acts.append(pltpu.make_async_copy(acts.at[rows], acts_v.at[rows], load_sem.at[2 + c]))
        load_grads.append(
            pltpu.make_async_copy(grads.at[rows], grads_v.at[rows], load_sem.at[2 + chunks + c])
        )
    small = [
        pltpu.make_async_copy(source, target, small_sem.at[n])
        for n, (source, target) in enumerate(
            ((lengths_in, lengths), (ids_in, ids), (slots_in, slots))
        )
    ]
    for copy in small:
        copy.start()
    load_w_in.start()
    for copy in load_acts:
        copy.start()
    load_w_out.start()
    for copy in load_grads:
        copy.start()

    barrier = pltpu.get_barrier_semaphore()
    for d in range(1, n_tp):
        pl.semaphore_signal(
            barrier, inc=1, device_id={"tp": lax.rem(tp + d, n_tp)}, device_id_type=MESH
        )
    for d in range(1, ranks):
        peer = lax.rem(rank + d, ranks)
        pl.semaphore_signal(
            barrier,
            inc=1,
            device_id={"seq": peer // n_sub, "sub": lax.rem(peer, n_sub)},
            device_id_type=MESH,
        )
    for copy in small:
        copy.wait()
    firsts = [jnp.int32(0)] * hard
    afters = [jnp.int32(0)] * hard
    chosen = [ids[0, k] for k in range(hard)]
    start = jnp.int32(0)
    for s in range(count):
        end = start + lengths[0, s]
        for k in range(hard):
            firsts[k] = jnp.where(chosen[k] == s, start, firsts[k])
            afters[k] = jnp.where(chosen[k] == s, end, afters[k])
        start = end
    tile_lane = lax.broadcasted_iota(jnp.int32, slot_all.shape[1:], 1)
    tile = jnp.full(slot_all.shape[1:], -1, jnp.int32)
    for k in range(hard):
        tile = jnp.where(tile_lane == rank * hard + k, slots[k], tile)
    slot_all[rank] = tile
    pl.semaphore_wait(barrier, n_tp - 1 + ranks - 1)

    slot_copies = []
    for d in range(1, ranks):
        peer = lax.rem(rank + d, ranks)
        copy = pltpu.make_async_remote_copy(
            src_ref=slot_all.at[rank],
            dst_ref=slot_all.at[rank],
            send_sem=s_send.at[d - 1],
            recv_sem=s_recv.at[d - 1],
            device_id={"seq": peer // n_sub, "sub": lax.rem(peer, n_sub)},
            device_id_type=MESH,
        )
        copy.start()
        slot_copies.append(copy)

    a_copies, g_copies = [], []
    load_w_in.wait()
    for c in range(chunks):
        load_acts[c].wait()
        part = project(acts_v[c * CHUNK:(c + 1) * CHUNK, :], w_in_v[...])
        turned = part.T
        for q in range(n_tp):
            a_own[c, q] = turned[q * share:(q + 1) * share, :]
        for d in range(1, n_tp):
            to = lax.rem(tp + d, n_tp)
            copy = pltpu.make_async_remote_copy(
                src_ref=a_own.at[c, to],
                dst_ref=a_got.at[d - 1, c],
                send_sem=a_send.at[d - 1, c],
                recv_sem=a_recv.at[d - 1, c],
                device_id={"tp": to},
                device_id_type=MESH,
            )
            copy.start()
            a_copies.append(copy)
    load_w_out.wait()
    for c in range(chunks):
        load_grads[c].wait()
        part = project(grads_v[c * CHUNK:(c + 1) * CHUNK, :], w_out_v[...])
        g_own[c] = jnp.concatenate([part[:half], part[half:]], axis=1)
        for d in range(1, n_tp):
            copy = pltpu.make_async_remote_copy(
                src_ref=g_own.at[c],
                dst_ref=g_got.at[d - 1, c],
                send_sem=g_send.at[d - 1, c],
                recv_sem=g_recv.at[d - 1, c],
                device_id={"tp": lax.rem(tp + d, n_tp)},
                device_id_type=MESH,
            )
            copy.start()
            g_copies.append(copy)

    for copy in slot_copies:
        copy.wait()
    every = slot_all[0]
    for other in range(1, ranks):
        every = jnp.maximum(every, slot_all[other])
    wanted = rank * hard + lax.broadcasted_iota(jnp.int32, every.shape, 0)
    picker = jnp.where(every == wanted, 1.0, 0.0)[:, :ranks * hard].astype(jnp.bfloat16)

    position = lax.broadcasted_iota(jnp.int32, (share, CHUNK), 1)
    lane = lax.broadcasted_iota(jnp.int32, (half, 2 * rank_full), 1)
    for c in range(chunks):
        for d in range(n_tp - 1):
            a_copies[c * (n_tp - 1) + d].wait()
        left = a_own[c, tp]
        for d in range(n_tp - 1):
            left = left + a_got[d, c]
        pieces = []
        for k in range(hard):
            inside = (position >= firsts[k] - c * CHUNK) & (position < afters[k] - c * CHUNK)
            pieces.append(jnp.where(inside, left, 0.0))
        left = jnp.concatenate(pieces, axis=0)
        left_hi = left.astype(jnp.bfloat16)
        left_lo = (left - left_hi.astype(jnp.float32)).astype(jnp.bfloat16)
        for d in range(n_tp - 1):
            g_copies[c * (n_tp - 1) + d].wait()
        pair = g_own[c]
        for d in range(n_tp - 1):
            pair = pair + g_got[d, c]
        swapped = pltpu.roll(pair, rank_full, 1)
        right = jnp.concatenate(
            [jnp.where(lane < rank_full, pair, swapped), jnp.where(lane < rank_full, swapped, pair)],
            axis=0,
        )
        right_hi = right.astype(jnp.bfloat16)
        right_lo = (right - right_hi.astype(jnp.float32)).astype(jnp.bfloat16)
        both = jnp.dot(
            left_hi,
            jnp.concatenate([right_hi, right_lo], axis=1),
            preferred_element_type=jnp.float32,
        )
        total = (
            both[:, :2 * rank_full]
            + both[:, 2 * rank_full:]
            + jnp.dot(left_lo, right_hi, preferred_element_type=jnp.float32)
        )
        if c == 0:
            acc[...] = total
        else:
            acc[...] += total
    out_lane = lax.broadcasted_iota(jnp.int32, (hard, 2 * rank_full), 1)
    mine = pl.ds(pl.multiple_of(rank * hard, hard), hard)
    for j in range(share // 2):
        even = acc[pl.ds(2 * j, hard, stride=share), :]
        odd = acc[pl.ds(2 * j + 1, hard, stride=share), :]
        gath[mine, j * 128:(j + 1) * 128] = jnp.where(out_lane < rank_full, even, odd)

    to_chips, to_cores = [], []
    for d in range(1, n_seq):
        copy = pltpu.make_async_remote_copy(
            src_ref=gath.at[mine],
            dst_ref=gath.at[mine],
            send_sem=f_send.at[d - 1],
            recv_sem=f_recv.at[d - 1],
            device_id={"seq": lax.rem(seq + d, n_seq)},
            device_id_type=MESH,
        )
        copy.start()
        to_chips.append(copy)
    for d in range(n_seq):
        if d:
            to_chips[d - 1].wait_recv()
        owner = lax.rem(seq + n_seq - d, n_seq) * n_sub + sub
        block = pl.ds(pl.multiple_of(owner * hard, hard), hard)
        for b in range(1, n_sub):
            copy = pltpu.make_async_remote_copy(
                src_ref=gath.at[block],
                dst_ref=gath.at[block],
                send_sem=h_send.at[b - 1, 0, d],
                recv_sem=h_send.at[b - 1, 1, d],
                device_id={"sub": lax.rem(sub + b, n_sub)},
                device_id_type=MESH,
            )
            copy.start()
            to_cores.append(copy)
    for copy in to_chips:
        copy.wait_send()
    for copy in to_cores:
        copy.wait()
    every = gath[...]
    high = every.astype(jnp.bfloat16)
    low = (every - high.astype(jnp.float32)).astype(jnp.bfloat16)
    out[...] = jnp.dot(picker, high, preferred_element_type=jnp.float32) + jnp.dot(
        picker, low, preferred_element_type=jnp.float32
    )


def body(acts, grads, w_in, w_out, lengths, ids, slots):
    n_seq, n_sub, n_tp = (lax.axis_size(name) for name in ("seq", "sub", "tp"))
    tokens, features = acts.shape
    hidden = grads.shape[1]
    rank_full = w_in.shape[1]
    w_in, w_out = w_in.T, w_out.T
    share = rank_full // n_tp
    hard = ids.shape[1]
    chunks = tokens // CHUNK
    ranks = n_seq * n_sub
    f32 = jnp.float32
    dma = pltpu.SemaphoreType.DMA
    hbm = pl.BlockSpec(memory_space=pltpu.HBM)

    def run(*refs):
        kernel(n_seq, n_sub, n_tp, *refs)

    return pl.pallas_call(
        run,
        out_shape=jax.ShapeDtypeStruct((hard, share * rank_full), f32),
        in_specs=[hbm] * 7,
        out_specs=pl.BlockSpec(memory_space=pltpu.VMEM),
        scratch_shapes=[
            pltpu.VMEM((tokens, features), acts.dtype),
            pltpu.VMEM((tokens, hidden), grads.dtype),
            pltpu.VMEM(w_in.shape, w_in.dtype),
            pltpu.VMEM(w_out.shape, w_out.dtype),
            pltpu.SMEM(lengths.shape, jnp.int32),
            pltpu.SMEM(ids.shape, jnp.int32),
            pltpu.SMEM(slots.shape, jnp.int32),
            pltpu.VMEM((chunks, n_tp, share, CHUNK), f32),
            pltpu.VMEM((n_tp - 1, chunks, share, CHUNK), f32),
            pltpu.VMEM((chunks, CHUNK // 2, 2 * rank_full), f32),
            pltpu.VMEM((n_tp - 1, chunks, CHUNK // 2, 2 * rank_full), f32),
            pltpu.VMEM((hard * share, 2 * rank_full), f32),
            pltpu.VMEM((ranks * hard, share * rank_full), f32),
            pltpu.VMEM((ranks, hard, -(-ranks * hard // 128) * 128), jnp.int32),
            dma((2 + 2 * chunks,)),
            dma((3,)),
            dma((n_tp - 1, chunks)),
            dma((n_tp - 1, chunks)),
            dma((n_tp - 1, chunks)),
            dma((n_tp - 1, chunks)),
            dma((ranks - 1,)),
            dma((ranks - 1,)),
            dma((n_seq - 1,)),
            dma((n_seq - 1,)),
            dma((n_sub - 1, 2, n_seq)),
        ],
        compiler_params=pltpu.CompilerParams(
            collective_id=0, has_side_effects=True, vmem_limit_bytes=60 * 2**20
        ),
        cost_estimate=pl.CostEstimate(
            flops=2 * tokens * (features + hidden) * rank_full,
            bytes_accessed=2 * tokens * (features + hidden),
            transcendentals=0,
        ),
    )(acts, grads, w_in, w_out, lengths, ids, slots)


def solution(mesh):
    placed = (
        P(("grp", "seq", "sub"), "tp"),
        P(("grp", "seq", "sub"), "tp"),
        P("tp", None),
        P("tp", None),
        P(("grp", "seq", "sub"), None),
        P(("grp", "seq", "sub"), None),
        P(("grp", "seq", "sub")),
    )
    return jax.shard_map(
        body, mesh=mesh, in_specs=placed, out_specs=P(("grp", "seq", "sub"), "tp"), check_vma=False
    )
```

```python
import jax
import jax.numpy as jnp
from jax import lax
from jax.experimental import pallas as pl
from jax.experimental.pallas import tpu as pltpu
from jax.sharding import PartitionSpec as P

MESH = pl.DeviceIdType.MESH
CHUNK = 256
AHEAD = 9
LOCAL = 0


def project(rows, turned):
    return lax.dot_general(
        rows, turned, (((1,), (1,)), ((), ())), preferred_element_type=jnp.float32
    )


def kernel(
    n_seq, n_sub, n_tp,
    acts, grads, w_in, w_out, lengths_in, ids_in, slots_in,
    out,
    acts_v, grads_v, w_in_v, w_out_v, lengths, ids, slots,
    a_own, a_got, g_own, g_got, acc, gath, slot_all,
    load_sem, small_sem, a_send, a_recv, g_send, g_recv, s_send, s_recv, f_send, f_recv, h_send,
):
    seq, sub, tp = lax.axis_index("seq"), lax.axis_index("sub"), lax.axis_index("tp")
    ranks = n_seq * n_sub
    rank = seq * n_sub + sub
    chunks = acts.shape[0] // CHUNK
    share = a_own.shape[2]
    hard = ids.shape[1]
    count = lengths.shape[1]
    half = CHUNK // 2
    rank_full = w_in.shape[0]

    load_w_in = pltpu.make_async_copy(w_in, w_in_v, load_sem.at[0])
    load_w_out = pltpu.make_async_copy(w_out, w_out_v, load_sem.at[1])
    load_acts = [
        pltpu.make_async_copy(
            acts.at[pl.ds(c * CHUNK, CHUNK)],
            acts_v.at[pl.ds(c * CHUNK, CHUNK)],
            load_sem.at[2 + c],
        )
        for c in range(chunks)
    ]
    load_grads = [
        pltpu.make_async_copy(
            grads.at[pl.ds(c * half, half)],
            grads_v.at[pl.ds(c * half, half)],
            load_sem.at[2 + chunks + c],
        )
        for c in range(2 * chunks)
    ]
    small = [
        pltpu.make_async_copy(source, target, small_sem.at[n])
        for n, (source, target) in enumerate(
            ((lengths_in, lengths), (ids_in, ids), (slots_in, slots))
        )
    ]
    for copy in small:
        copy.start()
    order = [load_w_in, *load_acts, load_w_out, *load_grads]
    for copy in order[:AHEAD]:
        copy.start()

    def take(n):
        order[n].wait()
        if n + AHEAD < len(order):
            order[n + AHEAD].start()


    barrier = pltpu.get_barrier_semaphore()
    for d in range(1, n_tp):
        pl.semaphore_signal(
            barrier, inc=1, device_id={"tp": lax.rem(tp + d, n_tp)}, device_id_type=MESH
        )
    for d in range(1, ranks):
        peer = lax.rem(rank + d, ranks)
        pl.semaphore_signal(
            barrier,
            inc=1,
            device_id={"seq": peer // n_sub, "sub": lax.rem(peer, n_sub)},
            device_id_type=MESH,
        )
    for copy in small:
        copy.wait()
    firsts = [jnp.int32(0)] * hard
    afters = [jnp.int32(0)] * hard
    chosen = [ids[0, k] for k in range(hard)]
    start = jnp.int32(0)
    for s in range(count):
        end = start + lengths[0, s]
        for k in range(hard):
            firsts[k] = jnp.where(chosen[k] == s, start, firsts[k])
            afters[k] = jnp.where(chosen[k] == s, end, afters[k])
        start = end
    tile_lane = lax.broadcasted_iota(jnp.int32, slot_all.shape[1:], 1)
    tile = jnp.full(slot_all.shape[1:], -1, jnp.int32)
    for k in range(hard):
        tile = jnp.where(tile_lane == rank * hard + k, slots[k], tile)
    slot_all[rank] = tile
    a_copies, g_copies, slot_copies = [], [], []

    def send_a(c):
        for d in range(1, n_tp):
            to = lax.rem(tp + d, n_tp)
            copy = pltpu.make_async_remote_copy(
                src_ref=a_own.at[c, to],
                dst_ref=a_got.at[d - 1, c],
                send_sem=a_send.at[d - 1, c],
                recv_sem=a_recv.at[d - 1, c],
                device_id={"tp": to},
                device_id_type=MESH,
            )
            copy.start()
            a_copies.append(copy)

    def send_g(c):
        for d in range(1, n_tp):
            copy = pltpu.make_async_remote_copy(
                src_ref=g_own.at[c],
                dst_ref=g_got.at[d - 1, c],
                send_sem=g_send.at[d - 1, c],
                recv_sem=g_recv.at[d - 1, c],
                device_id={"tp": lax.rem(tp + d, n_tp)},
                device_id_type=MESH,
            )
            copy.start()
            g_copies.append(copy)

    def enter():
        pl.semaphore_wait(barrier, n_tp - 1 + ranks - 1)
        for c in range(chunks):
            send_a(c)
        for c in range(LOCAL):
            send_g(c)
        for d in range(1, ranks):
            peer = lax.rem(rank + d, ranks)
            copy = pltpu.make_async_remote_copy(
                src_ref=slot_all.at[rank],
                dst_ref=slot_all.at[rank],
                send_sem=s_send.at[d - 1],
                recv_sem=s_recv.at[d - 1],
                device_id={"seq": peer // n_sub, "sub": lax.rem(peer, n_sub)},
                device_id_type=MESH,
            )
            copy.start()
            slot_copies.append(copy)

    take(0)
    for c in range(chunks):
        take(1 + c)
        turned = project(acts_v[c * CHUNK:(c + 1) * CHUNK, :], w_in_v[...]).T
        for q in range(n_tp):
            a_own[c, q] = turned[q * share:(q + 1) * share, :]
    take(1 + chunks)
    for c in range(chunks):
        if c == LOCAL:
            enter()
        for n in range(len(load_grads) // chunks):
            take(2 + chunks + c * (len(load_grads) // chunks) + n)
        part = project(grads_v[c * CHUNK:(c + 1) * CHUNK, :], w_out_v[...])
        g_own[c] = jnp.concatenate([part[:half], part[half:]], axis=1)
        if c >= LOCAL:
            send_g(c)

    for copy in slot_copies:
        copy.wait()
    every = slot_all[0]
    for other in range(1, ranks):
        every = jnp.maximum(every, slot_all[other])
    wanted = rank * hard + lax.broadcasted_iota(jnp.int32, every.shape, 0)
    picker = jnp.where(every == wanted, 1.0, 0.0)[:, :ranks * hard].astype(jnp.bfloat16)

    position = lax.broadcasted_iota(jnp.int32, (share, CHUNK), 1)
    lane = lax.broadcasted_iota(jnp.int32, (half, 2 * rank_full), 1)
    for c in range(chunks):
        for d in range(n_tp - 1):
            a_copies[c * (n_tp - 1) + d].wait()
        left = a_own[c, tp]
        for d in range(n_tp - 1):
            left = left + a_got[d, c]
        pieces = []
        for k in range(hard):
            inside = (position >= firsts[k] - c * CHUNK) & (position < afters[k] - c * CHUNK)
            pieces.append(jnp.where(inside, left, 0.0))
        left = jnp.concatenate(pieces, axis=0)
        left_hi = left.astype(jnp.bfloat16)
        left_lo = (left - left_hi.astype(jnp.float32)).astype(jnp.bfloat16)
        for d in range(n_tp - 1):
            g_copies[c * (n_tp - 1) + d].wait()
        pair = g_own[c]
        for d in range(n_tp - 1):
            pair = pair + g_got[d, c]
        swapped = pltpu.roll(pair, rank_full, 1)
        right = jnp.concatenate(
            [jnp.where(lane < rank_full, pair, swapped), jnp.where(lane < rank_full, swapped, pair)],
            axis=0,
        )
        right_hi = right.astype(jnp.bfloat16)
        right_lo = (right - right_hi.astype(jnp.float32)).astype(jnp.bfloat16)
        both = jnp.dot(
            left_hi,
            jnp.concatenate([right_hi, right_lo], axis=1),
            preferred_element_type=jnp.float32,
        )
        total = (
            both[:, :2 * rank_full]
            + both[:, 2 * rank_full:]
            + jnp.dot(left_lo, right_hi, preferred_element_type=jnp.float32)
        )
        if c == 0:
            acc[...] = total
        else:
            acc[...] += total
    out_lane = lax.broadcasted_iota(jnp.int32, (hard, 2 * rank_full), 1)
    mine = pl.ds(pl.multiple_of(rank * hard, hard), hard)
    for j in range(share // 2):
        even = acc[pl.ds(2 * j, hard, stride=share), :]
        odd = acc[pl.ds(2 * j + 1, hard, stride=share), :]
        gath[mine, j * 128:(j + 1) * 128] = jnp.where(out_lane < rank_full, even, odd)

    to_chips, to_cores = [], []
    for d in range(1, n_seq):
        copy = pltpu.make_async_remote_copy(
            src_ref=gath.at[mine],
            dst_ref=gath.at[mine],
            send_sem=f_send.at[d - 1],
            recv_sem=f_recv.at[d - 1],
            device_id={"seq": lax.rem(seq + d, n_seq)},
            device_id_type=MESH,
        )
        copy.start()
        to_chips.append(copy)
    for d in range(n_seq):
        if d:
            to_chips[d - 1].wait_recv()
        owner = lax.rem(seq + n_seq - d, n_seq) * n_sub + sub
        block = pl.ds(pl.multiple_of(owner * hard, hard), hard)
        for b in range(1, n_sub):
            copy = pltpu.make_async_remote_copy(
                src_ref=gath.at[block],
                dst_ref=gath.at[block],
                send_sem=h_send.at[b - 1, 0, d],
                recv_sem=h_send.at[b - 1, 1, d],
                device_id={"sub": lax.rem(sub + b, n_sub)},
                device_id_type=MESH,
            )
            copy.start()
            to_cores.append(copy)
    for copy in to_chips:
        copy.wait_send()
    for copy in to_cores:
        copy.wait()
    every = gath[...]
    high = every.astype(jnp.bfloat16)
    low = (every - high.astype(jnp.float32)).astype(jnp.bfloat16)
    out[...] = jnp.dot(picker, high, preferred_element_type=jnp.float32) + jnp.dot(
        picker, low, preferred_element_type=jnp.float32
    )


def body(acts, grads, w_in, w_out, lengths, ids, slots):
    n_seq, n_sub, n_tp = (lax.axis_size(name) for name in ("seq", "sub", "tp"))
    tokens, features = acts.shape
    hidden = grads.shape[1]
    rank_full = w_in.shape[1]
    w_in, w_out = w_in.T, w_out.T
    share = rank_full // n_tp
    hard = ids.shape[1]
    chunks = tokens // CHUNK
    ranks = n_seq * n_sub
    f32 = jnp.float32
    dma = pltpu.SemaphoreType.DMA
    hbm = pl.BlockSpec(memory_space=pltpu.HBM)

    def run(*refs):
        kernel(n_seq, n_sub, n_tp, *refs)

    return pl.pallas_call(
        run,
        out_shape=jax.ShapeDtypeStruct((hard, share * rank_full), f32),
        in_specs=[hbm] * 7,
        out_specs=pl.BlockSpec(memory_space=pltpu.VMEM),
        scratch_shapes=[
            pltpu.VMEM((tokens, features), acts.dtype),
            pltpu.VMEM((tokens, hidden), grads.dtype),
            pltpu.VMEM(w_in.shape, w_in.dtype),
            pltpu.VMEM(w_out.shape, w_out.dtype),
            pltpu.SMEM(lengths.shape, jnp.int32),
            pltpu.SMEM(ids.shape, jnp.int32),
            pltpu.SMEM(slots.shape, jnp.int32),
            pltpu.VMEM((chunks, n_tp, share, CHUNK), f32),
            pltpu.VMEM((n_tp - 1, chunks, share, CHUNK), f32),
            pltpu.VMEM((chunks, CHUNK // 2, 2 * rank_full), f32),
            pltpu.VMEM((n_tp - 1, chunks, CHUNK // 2, 2 * rank_full), f32),
            pltpu.VMEM((hard * share, 2 * rank_full), f32),
            pltpu.VMEM((ranks * hard, share * rank_full), f32),
            pltpu.VMEM((ranks, hard, -(-ranks * hard // 128) * 128), jnp.int32),
            dma((2 + 3 * chunks,)),
            dma((3,)),
            dma((n_tp - 1, chunks)),
            dma((n_tp - 1, chunks)),
            dma((n_tp - 1, chunks)),
            dma((n_tp - 1, chunks)),
            dma((ranks - 1,)),
            dma((ranks - 1,)),
            dma((n_seq - 1,)),
            dma((n_seq - 1,)),
            dma((n_sub - 1, 2, n_seq)),
        ],
        compiler_params=pltpu.CompilerParams(
            collective_id=0, has_side_effects=True, vmem_limit_bytes=60 * 2**20
        ),
        cost_estimate=pl.CostEstimate(
            flops=2 * tokens * (features + hidden) * rank_full,
            bytes_accessed=2 * tokens * (features + hidden),
            transcendentals=0,
        ),
    )(acts, grads, w_in, w_out, lengths, ids, slots)


def solution(mesh):
    placed = (
        P(("grp", "seq", "sub"), "tp"),
        P(("grp", "seq", "sub"), "tp"),
        P("tp", None),
        P("tp", None),
        P(("grp", "seq", "sub"), None),
        P(("grp", "seq", "sub"), None),
        P(("grp", "seq", "sub")),
    )
    return jax.shard_map(
        body, mesh=mesh, in_specs=placed, out_specs=P(("grp", "seq", "sub"), "tp"), check_vma=False
    )
```
